512 devices in a mesh: grp: 16 (over z_lo, x), mem: 32 (over y, z_hi, core).
Axes of the slice: x: 4, y: 8, z: 8 (z_hi: 2, z_lo: 4; z = z_hi * 4 + z_lo), core: 2. Of those that a mesh axis runs over, the one named last changes fastest.
Arguments:
- points: float32 [8192, 128], P(('grp', 'mem')), may hold values from -40 to 40, as said below
- slab: float32 [65536, 128], P('mem'), may hold values from -40 to 40, as said below
Outputs:
- new_points: float32 [8192, 128], P(('grp', 'mem'))
The draws below stay inside these ranges and needn't reach their ends.
Inputs may be any that keep to these rules, and one draw needn't show every extreme that they name: Support points lie near the chains' centres. `slab`: each block of 2048 rows is one chain with its own centre and scale.
All inputs are finite; a program needn't handle non-finite values.
Results may differ from the reference program's by a relative error of at most 0.0001.
Values sent between devices are 32-bit elements; how exact they have to be, the bound alone decides.
No kernel may reach another device: no remote copies, remote signals or barrier semaphores. Data moves between devices by JAX's collectives and lax.ppermute only.
A program may use at most 64 MiB of HBM per device.

```python
import jax
import jax.numpy as jnp
from jax import lax

D = 128
PT_DEV = 16
SAMP_DEV = 2048
NPTS = 8192
NSAMP = 65536
N_GRP = 16
N_MEM = 32


def chain_centres(key):
    return 1.5 * jax.random.normal(jax.random.fold_in(key, 7), (N_MEM, D), jnp.float32)


def draw_slab(key, part):
    centres = chain_centres(key)
    scales = jnp.exp(jax.random.uniform(jax.random.fold_in(key, 11), (N_MEM,), jnp.float32, -0.7, 0.7))
    noise = jax.random.normal(jax.random.fold_in(key, 13), (N_MEM, SAMP_DEV, D), jnp.float32)
    values = centres[:, None, :] + scales[:, None, None] * noise
    return jnp.clip(values, -40.0, 40.0).reshape(N_MEM * SAMP_DEV, D)


def draw_points(key, part):
    centres = chain_centres(key)
    count = PT_DEV * N_GRP * N_MEM
    which = jax.random.randint(jax.random.fold_in(key, 19), (count,), 0, N_MEM)
    onehot = (which[:, None] == jnp.arange(N_MEM)[None, :]).astype(jnp.float32)
    noise = jax.random.normal(jax.random.fold_in(key, 23), (count, D), jnp.float32)
    values = jnp.dot(onehot, centres) + noise
    return jnp.clip(values, -40.0, 40.0)


def setup_inputs(seed: int = 0) -> dict:
    splits = jax.random.split(jax.random.key(seed), 3)
    return {
        "points": draw_points(jax.random.fold_in(splits[2], 71), 0),
        "slab": draw_slab(jax.random.fold_in(splits[2], 71), 0),
    }


def weights_of(left, right_operand):
    left_square_norm = lax.optimization_barrier(jnp.sum(jnp.square(left), axis=1))
    right_square_norm = lax.optimization_barrier(jnp.sum(jnp.square(right_operand), axis=1))
    cross_product = jnp.dot(left, right_operand.T, precision=lax.Precision.HIGHEST, preferred_element_type=jnp.float32)
    squared_distance = left_square_norm[:, None] + right_square_norm[None, :] - 2.0 * cross_product
    return 1.0 / jnp.sqrt(squared_distance + 1.0)

def reference(points, slab):
    ratio = NSAMP / NPTS
    support_point_block = min(NPTS, 512)
    sblock = min(NSAMP, 512)
    slab_blocks = slab.reshape(NSAMP // sblock, sblock, D)

    def one_block(block):

        def step(carry, rows):
            numer, total = carry
            wts = weights_of(block, rows)
            numer = numer + jnp.dot(wts, rows, precision=lax.Precision.HIGHEST, preferred_element_type=jnp.float32)
            total = total + lax.optimization_barrier(jnp.sum(wts, axis=1))
            return ((numer, total), None)
        init = (jnp.zeros((support_point_block, D), jnp.float32), jnp.zeros((support_point_block,), jnp.float32))
        (numer, total), _ = lax.scan(step, init, slab_blocks)
        pw = weights_of(block, points)
        pair_vec = jnp.dot(pw, points, precision=lax.Precision.HIGHEST, preferred_element_type=jnp.float32)
        pair_sum = lax.optimization_barrier(jnp.sum(pw, axis=1))
        repel = block * pair_sum[:, None] - pair_vec
        return (ratio * repel + numer) / total[:, None]
    update_output = lax.map(one_block, points.reshape(NPTS // support_point_block, support_point_block, D))
    return update_output.reshape(NPTS, D)
```

```python
import functools

import jax
import jax.numpy as jnp
from jax import lax
from jax.experimental import pallas as pl
from jax.experimental.pallas import tpu as pltpu
from jax.sharding import PartitionSpec as P

F32, BF16 = jnp.float32, jnp.bfloat16
AXES = ("grp", "mem")
CHIPS_X, CHIPS_Y, Z_LO, Z_HI, CORES = 4, 8, 4, 2, 2
TILE = 512


def place(index):
    group, member = divmod(index, CHIPS_Y * Z_HI * CORES)
    z_lo, x = divmod(group, CHIPS_X)
    y, rest = divmod(member, Z_HI * CORES)
    z_hi, core = divmod(rest, CORES)
    return x, y, z_hi * Z_LO + z_lo, core


def index_of(x, y, z, core):
    z_hi, z_lo = divmod(z, Z_LO)
    return (z_lo * CHIPS_X + x) * CHIPS_Y * Z_HI * CORES + (y * Z_HI + z_hi) * CORES + core


def team_of(z):
    return z if z < Z_LO else (z - Z_LO) ^ 2


DEVICES = range(CHIPS_X * CHIPS_Y * Z_LO * Z_HI * CORES)
TEAMS = {}
for _i in DEVICES:
    _x, _y, _z, _c = place(_i)
    TEAMS.setdefault((_x, team_of(_z), _c), []).append(_i)
TEAMS = list(TEAMS.values())

Z_ORDER = ((0, 2, 1, 3, 4, 6, 5, 7), (1, 0, 3, 2, 6, 7, 4, 5))
CROSS = []
for _i in DEVICES:
    _x, _y, _z, _c = place(_i)
    CROSS.append((index_of((_x + _y) % CHIPS_X, _y, Z_ORDER[_y // CHIPS_X][_z], _c), _i))
SWAP = [(i, i ^ 1) for i in DEVICES]


def split2(v):
    hi = v.astype(BF16)
    return hi, (v - hi.astype(F32)).astype(BF16)


def split3(v):
    hi = v.astype(BF16).astype(F32)
    mid = (v - hi).astype(BF16).astype(F32)
    return hi, mid, v - hi - mid


def columns(first, second):
    ref = second if first is None else first
    lane = lax.broadcasted_iota(jnp.int32, (ref.shape[0], 128), 1)
    out = jnp.where(lane < 6, 1.0, 0.0).astype(F32)
    for at, col in ((0, first), (3, second)):
        if col is not None:
            for k, part in enumerate(split3(col)):
                out = jnp.where(lane == at + k, part, out)
    return out.astype(BF16)


NT = (((1,), (1,)), ((), ()))


def left_operands(pts):
    hi, lo = split2(-2.0 * pts)
    norm = jnp.sum(pts * pts, axis=1, keepdims=True) + 1.0
    return jnp.concatenate([hi, hi], axis=1), jnp.concatenate([lo, columns(None, norm)], axis=1)


def accumulate(left, rows, state):
    vec, tot = state
    hi, lo = split2(rows)
    norm = jnp.sum(rows * rows, axis=1, keepdims=True)
    both = jnp.concatenate([hi, lo], axis=1)
    extra = jnp.concatenate([hi, columns(norm, None)], axis=1)
    d = lax.dot_general(left[0], both, NT, preferred_element_type=F32)
    d = d + lax.dot_general(left[1], extra, NT, preferred_element_type=F32)
    w = lax.rsqrt(jnp.maximum(d, 1.0))
    w_hi, w_lo = split2(w)
    part = jnp.dot(w_hi, both, preferred_element_type=F32)
    part = part + jnp.dot(w_lo, both, preferred_element_type=F32)
    vec = vec + part
    for k in range(rows.shape[0] // 128):
        tot = tot + w[:, 128 * k : 128 * (k + 1)]
    return vec, tot


def slab_kernel(pts_ref, own_ref, other_ref, vec_ref, tot_ref):
    pts = pts_ref[...]
    left = left_operands(pts)
    state = (jnp.zeros((pts.shape[0], 256), F32), jnp.zeros((pts.shape[0], 128), F32))
    for ref in (own_ref, other_ref):
        for t in range(ref.shape[0] // TILE):
            state = accumulate(left, ref[t * TILE : (t + 1) * TILE, :], state)
    vec_ref[...] = state[0][:, :128] + state[0][:, 128:]
    tot_ref[...] = state[1]


def pair_kernel(ratio, pts_ref, first_ref, second_ref, vec_ref, tot_ref, out_ref):
    pts = pts_ref[...]
    left = left_operands(pts)
    state = (jnp.zeros((pts.shape[0], 256), F32), jnp.zeros((pts.shape[0], 128), F32))
    for ref in (first_ref, second_ref):
        state = accumulate(left, ref[...], state)
    pair_sum = jnp.sum(state[1], axis=1, keepdims=True)
    repel = pts * pair_sum - (state[0][:, :128] + state[0][:, 128:])
    numer = ratio * repel + vec_ref[...]
    weight = jnp.sum(tot_ref[...], axis=1, keepdims=True)
    lane = lax.broadcasted_iota(jnp.int32, (8, 128), 1)
    for k in range(out_ref.shape[0]):
        at = 16 * k
        out_ref[k, 0:16, :] = numer[at : at + 16]
        out_ref[k, 16:24, :] = jnp.where(lane < 64, weight[at : at + 8], weight[at + 8 : at + 16])


def final_kernel(parts_ref, out_ref):
    total = parts_ref[0]
    for k in range(1, parts_ref.shape[0]):
        total = total + parts_ref[k]
    out_ref[0:8, :] = total[0:8] / total[16:24, 0:1]
    out_ref[8:16, :] = total[8:16] / total[16:24, 127:128]


def call(kernel, shapes, flops, *args):
    return pl.pallas_call(
        kernel,
        out_shape=shapes,
        in_specs=[pl.BlockSpec(memory_space=pltpu.VMEM)] * len(args),
        out_specs=jax.tree.map(lambda _: pl.BlockSpec(memory_space=pltpu.VMEM), shapes),
        cost_estimate=pl.CostEstimate(flops=flops, bytes_accessed=1 << 20, transcendentals=1 << 20),
        compiler_params=pltpu.CompilerParams(vmem_limit_bytes=48 << 20),
    )(*args)


def shards(points, slab):
    owned, width = points.shape
    team = len(TEAMS[0])
    ratio = slab.shape[0] / (owned * lax.axis_size("grp"))
    other = lax.ppermute(slab, AXES, SWAP)
    copies = jnp.broadcast_to(points[None], (team, owned, width))
    pts = lax.all_to_all(copies, AXES, 0, 0, axis_index_groups=TEAMS).reshape(team * owned, width)
    far = lax.ppermute(pts, AXES, CROSS)
    sums = (
        jax.ShapeDtypeStruct((team * owned, width), F32),
        jax.ShapeDtypeStruct((team * owned, 128), F32),
    )
    vec, tot = call(slab_kernel, sums, 1 << 32, pts, slab, other)
    far_other = lax.ppermute(far, AXES, SWAP)
    block = jax.ShapeDtypeStruct((team, owned + 8, width), F32)
    part = call(functools.partial(pair_kernel, ratio), block, 1 << 28, pts, far, far_other, vec, tot)
    parts = lax.all_to_all(part, AXES, 0, 0, axis_index_groups=TEAMS)
    return call(final_kernel, jax.ShapeDtypeStruct((owned, width), F32), 1 << 16, parts)


def solution(mesh):
    placed = (P(("grp", "mem"), None), P("mem", None))
    return jax.shard_map(
        shards, mesh=mesh, in_specs=placed, out_specs=P(("grp", "mem"), None), check_vma=False
    )
```

```python
import functools

import jax
import jax.numpy as jnp
from jax import lax
from jax.experimental import pallas as pl
from jax.experimental.pallas import tpu as pltpu
from jax.sharding import PartitionSpec as P

F32, BF16 = jnp.float32, jnp.bfloat16
AXES = ("grp", "mem")
CHIPS_X, CHIPS_Y, Z_LO, Z_HI, CORES = 4, 8, 4, 2, 2
TILE = 512
HEAD = 1
COST = (1 << 20, 1 << 34, 1 << 31)


def place(index):
    group, member = divmod(index, CHIPS_Y * Z_HI * CORES)
    z_lo, x = divmod(group, CHIPS_X)
    y, rest = divmod(member, Z_HI * CORES)
    z_hi, core = divmod(rest, CORES)
    return x, y, z_hi * Z_LO + z_lo, core


def index_of(x, y, z, core):
    z_hi, z_lo = divmod(z, Z_LO)
    return (z_lo * CHIPS_X + x) * CHIPS_Y * Z_HI * CORES + (y * Z_HI + z_hi) * CORES + core


def team_of(z):
    return z if z < Z_LO else (z - Z_LO) ^ 2


DEVICES = range(CHIPS_X * CHIPS_Y * Z_LO * Z_HI * CORES)
TEAMS = {}
for _i in DEVICES:
    _x, _y, _z, _c = place(_i)
    TEAMS.setdefault((_x, team_of(_z), _c), []).append(_i)
TEAMS = list(TEAMS.values())

Z_ORDER = ((0, 2, 1, 3, 4, 6, 5, 7), (1, 0, 3, 2, 6, 7, 4, 5))
CROSS = []
for _i in DEVICES:
    _x, _y, _z, _c = place(_i)
    CROSS.append((index_of((_x + _y) % CHIPS_X, _y, Z_ORDER[_y // CHIPS_X][_z], _c), _i))
SWAP = [(i, i ^ 1) for i in DEVICES]


def split2(v):
    hi = v.astype(BF16)
    return hi, (v - hi.astype(F32)).astype(BF16)


def split3(v):
    hi = v.astype(BF16).astype(F32)
    mid = (v - hi).astype(BF16).astype(F32)
    return hi, mid, v - hi - mid


def columns(first, second):
    ref = second if first is None else first
    lane = lax.broadcasted_iota(jnp.int32, (ref.shape[0], 128), 1)
    out = jnp.where(lane < 6, 1.0, 0.0).astype(F32)
    for at, col in ((0, first), (3, second)):
        if col is not None:
            for k, part in enumerate(split3(col)):
                out = jnp.where(lane == at + k, part, out)
    return out.astype(BF16)


NT = (((1,), (1,)), ((), ()))


def left_operands(pts):
    hi, lo = split2(-2.0 * pts)
    norm = jnp.sum(pts * pts, axis=1, keepdims=True) + 1.0
    return jnp.concatenate([hi, hi], axis=1), jnp.concatenate([lo, columns(None, norm)], axis=1)


def accumulate(left, rows, state):
    vec, tot = state
    hi, lo = split2(rows)
    norm = jnp.sum(rows * rows, axis=1, keepdims=True)
    both = jnp.concatenate([hi, lo], axis=1)
    extra = jnp.concatenate([hi, columns(norm, None)], axis=1)
    d = lax.dot_general(left[0], both, NT, preferred_element_type=F32)
    d = d + lax.dot_general(left[1], extra, NT, preferred_element_type=F32)
    w = lax.rsqrt(jnp.maximum(d, 1.0))
    w_hi, w_lo = split2(w)
    part = jnp.dot(w_hi, both, preferred_element_type=F32)
    part = part + jnp.dot(w_lo, both, preferred_element_type=F32)
    vec = vec + part
    for k in range(rows.shape[0] // 128):
        tot = tot + w[:, 128 * k : 128 * (k + 1)]
    return vec, tot


def zeros(rows):
    return jnp.zeros((rows, 256), F32), jnp.zeros((rows, 128), F32)


def add_tiles(left, state, slab_ref, tiles):
    for t in tiles:
        state = accumulate(left, slab_ref[t * TILE : (t + 1) * TILE, :], state)
    return state


def head_kernel(pts_ref, slab_ref, left1_ref, left2_ref, vec_ref, tot_ref, held, sem):
    copy = pltpu.make_async_copy(slab_ref.at[pl.ds(0, held.shape[0])], held, sem)
    copy.start()
    pts = pts_ref[...]
    left = left_operands(pts)
    left1_ref[...], left2_ref[...] = left
    copy.wait()
    vec_ref[...], tot_ref[...] = add_tiles(left, zeros(pts.shape[0]), held, range(HEAD))


def rest_kernel(first, left1_ref, left2_ref, vec_in, tot_in, slab_ref, vec_ref, tot_ref):
    left, state = (left1_ref[...], left2_ref[...]), (vec_in[...], tot_in[...])
    tiles = range(first, slab_ref.shape[0] // TILE)
    vec_ref[...], tot_ref[...] = add_tiles(left, state, slab_ref, tiles)


def pair_kernel(ratio, pts_ref, left1_ref, left2_ref, first_ref, second_ref, vec_ref, tot_ref, out_ref):
    pts = pts_ref[...]
    left = left1_ref[...], left2_ref[...]
    state = zeros(pts.shape[0])
    for ref in (first_ref, second_ref):
        state = accumulate(left, ref[...], state)
    pair_sum = jnp.sum(state[1], axis=1, keepdims=True)
    repel = pts * pair_sum - (state[0][:, :128] + state[0][:, 128:])
    numer = ratio * repel + (vec_ref[:, :128] + vec_ref[:, 128:])
    weight = jnp.sum(tot_ref[...], axis=1, keepdims=True)
    lane = lax.broadcasted_iota(jnp.int32, (8, 128), 1)
    for k in range(out_ref.shape[0]):
        at = 16 * k
        out_ref[k, 0:16, :] = numer[at : at + 16]
        out_ref[k, 16:24, :] = jnp.where(lane < 64, weight[at : at + 8], weight[at + 8 : at + 16])


def final_kernel(parts_ref, out_ref):
    total = parts_ref[0]
    for k in range(1, parts_ref.shape[0]):
        total = total + parts_ref[k]
    out_ref[0:8, :] = total[0:8] / total[16:24, 0:1]
    out_ref[8:16, :] = total[8:16] / total[16:24, 127:128]


def call(kernel, shapes, flops, *args, hbm=(), scratch=()):
    args = [pltpu.with_memory_space_constraint(a, pltpu.HBM) if k in hbm else a for k, a in enumerate(args)]
    spaces = [pltpu.HBM if k in hbm else pltpu.VMEM for k in range(len(args))]
    return pl.pallas_call(
        kernel,
        out_shape=shapes,
        in_specs=[pl.BlockSpec(memory_space=space) for space in spaces],
        out_specs=jax.tree.map(lambda _: pl.BlockSpec(memory_space=pltpu.VMEM), shapes),
        scratch_shapes=scratch,
        cost_estimate=pl.CostEstimate(flops=flops, bytes_accessed=1 << 10, transcendentals=1),
        compiler_params=pltpu.CompilerParams(vmem_limit_bytes=24 << 20),
    )(*args)


def shards(points, slab):
    owned, width = points.shape
    team = len(TEAMS[0])
    ratio = slab.shape[0] / (owned * lax.axis_size("grp"))
    copies = jnp.broadcast_to(points[None], (team, owned, width))
    pts = lax.all_to_all(copies, AXES, 0, 0, axis_index_groups=TEAMS).reshape(team * owned, width)
    far = lax.ppermute(pts, AXES, CROSS)
    rows = team * owned
    half = jax.ShapeDtypeStruct((rows, 256), BF16)
    wide = jax.ShapeDtypeStruct((rows, 256), F32)
    narrow = jax.ShapeDtypeStruct((rows, 128), F32)

    held = [pltpu.VMEM((HEAD * TILE, width), F32), pltpu.SemaphoreType.DMA]
    first = functools.partial(rest_kernel, HEAD)
    second = functools.partial(rest_kernel, 0)
    *left, vec, tot = call(head_kernel, (half, half, wide, narrow), COST[0], pts, slab, hbm=(1,), scratch=held)
    slab_later, _ = lax.optimization_barrier((slab, tot))
    other = lax.ppermute(slab_later, AXES, SWAP)
    vec, tot = call(first, (wide, narrow), COST[1], *left, vec, tot, slab)
    far, _ = lax.optimization_barrier((far, tot))
    far_other = lax.ppermute(far, AXES, SWAP)
    vec, tot = call(second, (wide, narrow), COST[2], *left, vec, tot, other)
    block = jax.ShapeDtypeStruct((team, owned + 8, width), F32)
    pair = functools.partial(pair_kernel, ratio)
    part = call(pair, block, 1 << 28, pts, *left, far, far_other, vec, tot)
    parts = lax.all_to_all(part, AXES, 0, 0, axis_index_groups=TEAMS)
    return call(final_kernel, jax.ShapeDtypeStruct((owned, width), F32), 1 << 16, parts)


def solution(mesh):
    placed = (P(("grp", "mem"), None), P("mem", None))
    return jax.shard_map(
        shards, mesh=mesh, in_specs=placed, out_specs=P(("grp", "mem"), None), check_vma=False
    )
```

```python
import functools

import jax
import jax.numpy as jnp
from jax import lax
from jax.experimental import pallas as pl
from jax.experimental.pallas import tpu as pltpu
from jax.sharding import PartitionSpec as P

F32, BF16 = jnp.float32, jnp.bfloat16
AXES = ("grp", "mem")
CHIPS_X, CHIPS_Y, Z_LO, Z_HI, CORES = 4, 8, 4, 2, 2
TILE = 512
COST = (1 << 34, 1 << 31)


def place(index):
    group, member = divmod(index, CHIPS_Y * Z_HI * CORES)
    z_lo, x = divmod(group, CHIPS_X)
    y, rest = divmod(member, Z_HI * CORES)
    z_hi, core = divmod(rest, CORES)
    return x, y, z_hi * Z_LO + z_lo, core


def index_of(x, y, z, core):
    z_hi, z_lo = divmod(z, Z_LO)
    return (z_lo * CHIPS_X + x) * CHIPS_Y * Z_HI * CORES + (y * Z_HI + z_hi) * CORES + core


def team_of(z):
    return z if z < Z_LO else (z - Z_LO) ^ 2


DEVICES = range(CHIPS_X * CHIPS_Y * Z_LO * Z_HI * CORES)
TEAMS = {}
for _i in DEVICES:
    _x, _y, _z, _c = place(_i)
    TEAMS.setdefault((_x, team_of(_z), _c), []).append(_i)
TEAMS = list(TEAMS.values())

X_ORDER = ((2, 1, 0, 3), (1, 2, 3, 0), (0, 3, 2, 1), (3, 0, 1, 2))
Z_ORDER = ((0, 2, 1, 3, 4, 6, 5, 7), (1, 3, 0, 2, 5, 7, 4, 6))
CROSS = []
for _i in DEVICES:
    _x, _y, _z, _c = place(_i)
    _far = X_ORDER[_y % CHIPS_X][_x], _y, Z_ORDER[_y // CHIPS_X][_z], _c
    CROSS.append((index_of(*_far), _i))
SWAP = [(i, i ^ 1) for i in DEVICES]


def split2(v):
    hi = v.astype(BF16)
    return hi, (v - hi.astype(F32)).astype(BF16)


def split3(v):
    hi = v.astype(BF16).astype(F32)
    mid = (v - hi).astype(BF16).astype(F32)
    return hi, mid, v - hi - mid


def columns(first, second):
    ref = second if first is None else first
    lane = lax.broadcasted_iota(jnp.int32, (ref.shape[0], 128), 1)
    out = jnp.where(lane < 6, 1.0, 0.0).astype(F32)
    for at, col in ((0, first), (3, second)):
        if col is not None:
            for k, part in enumerate(split3(col)):
                out = jnp.where(lane == at + k, part, out)
    return out.astype(BF16)


NT = (((1,), (1,)), ((), ()))


def left_operands(pts):
    hi, lo = split2(-2.0 * pts)
    norm = jnp.sum(pts * pts, axis=1, keepdims=True) + 1.0
    return jnp.concatenate([hi, hi], axis=1), jnp.concatenate([lo, columns(None, norm)], axis=1)


def accumulate(left, rows, state):
    vec, tot = state
    hi, lo = split2(rows)
    norm = jnp.sum(rows * rows, axis=1, keepdims=True)
    both = jnp.concatenate([hi, lo], axis=1)
    extra = jnp.concatenate([hi, columns(norm, None)], axis=1)
    d = lax.dot_general(left[0], both, NT, preferred_element_type=F32)
    d = d + lax.dot_general(left[1], extra, NT, preferred_element_type=F32)
    w = lax.rsqrt(jnp.maximum(d, 1.0))
    w_hi, w_lo = split2(w)
    part = jnp.dot(w_hi, both, preferred_element_type=F32)
    part = part + jnp.dot(w_lo, both, preferred_element_type=F32)
    vec = vec + part
    for k in range(rows.shape[0] // 128):
        tot = tot + w[:, 128 * k : 128 * (k + 1)]
    return vec, tot


def zeros(rows):
    return jnp.zeros((rows, 256), F32), jnp.zeros((rows, 128), F32)


def add_tiles(left, state, slab_ref, tiles):
    for t in tiles:
        state = accumulate(left, slab_ref[t * TILE : (t + 1) * TILE, :], state)
    return state


def own_kernel(pts_ref, slab_ref, left1_ref, left2_ref, vec_ref, tot_ref, held, sems):
    copies = [
        pltpu.make_async_copy(slab_ref.at[pl.ds(t * TILE, TILE)], held.at[t], sems.at[t])
        for t in range(held.shape[0])
    ]
    for copy in copies:
        copy.start()
    left = left_operands(pts_ref[...])
    left1_ref[...], left2_ref[...] = left
    state = zeros(pts_ref.shape[0])
    for t, copy in enumerate(copies):
        copy.wait()
        state = accumulate(left, held[t], state)
    vec_ref[...], tot_ref[...] = state


def other_kernel(left1_ref, left2_ref, vec_in, tot_in, slab_ref, vec_ref, tot_ref):
    left, state = (left1_ref[...], left2_ref[...]), (vec_in[...], tot_in[...])
    for t in range(slab_ref.shape[0] // TILE):
        state = accumulate(left, slab_ref[t * TILE : (t + 1) * TILE, :], state)
    vec_ref[...], tot_ref[...] = state


def pair_kernel(ratio, pts_ref, left1_ref, left2_ref, first_ref, second_ref, vec_ref, tot_ref, out_ref):
    pts = pts_ref[...]
    left = left1_ref[...], left2_ref[...]
    state = zeros(pts.shape[0])
    for ref in (first_ref, second_ref):
        state = accumulate(left, ref[...], state)
    pair_sum = jnp.sum(state[1], axis=1, keepdims=True)
    repel = pts * pair_sum - (state[0][:, :128] + state[0][:, 128:])
    numer = ratio * repel + (vec_ref[:, :128] + vec_ref[:, 128:])
    weight = jnp.sum(tot_ref[...], axis=1, keepdims=True)
    spread = jnp.where(lax.broadcasted_iota(jnp.int32, (256, 128), 0) % 16 == lax.broadcasted_iota(jnp.int32, (256, 128), 1), weight, 0.0)
    for k in range(out_ref.shape[0]):
        at = 16 * k
        out_ref[k, 0:16, 0, :] = numer[at : at + 16]
        out_ref[k, 16, 0, :] = jnp.sum(spread[at : at + 16], axis=0)


def final_kernel(parts_ref, out_ref):
    total = parts_ref[0, :, 0, :]
    for k in range(1, parts_ref.shape[0]):
        total = total + parts_ref[k, :, 0, :]
    rows = lax.broadcasted_iota(jnp.int32, (16, 128), 0)
    lanes = lax.broadcasted_iota(jnp.int32, (16, 128), 1)
    weight = jnp.sum(jnp.where(rows == lanes, total[16:17], 0.0), axis=1, keepdims=True)
    out_ref[...] = total[0:16] / weight


def call(kernel, shapes, flops, *args, hbm=(), scratch=()):
    args = [pltpu.with_memory_space_constraint(a, pltpu.HBM) if k in hbm else a for k, a in enumerate(args)]
    spaces = [pltpu.HBM if k in hbm else pltpu.VMEM for k in range(len(args))]
    return pl.pallas_call(
        kernel,
        out_shape=shapes,
        in_specs=[pl.BlockSpec(memory_space=space) for space in spaces],
        out_specs=jax.tree.map(lambda _: pl.BlockSpec(memory_space=pltpu.VMEM), shapes),
        scratch_shapes=scratch,
        cost_estimate=pl.CostEstimate(flops=flops, bytes_accessed=1 << 10, transcendentals=1),
        compiler_params=pltpu.CompilerParams(vmem_limit_bytes=24 << 20),
    )(*args)


def shards(points, slab):
    owned, width = points.shape
    team = len(TEAMS[0])
    ratio = slab.shape[0] / (owned * lax.axis_size("grp"))
    copies = jnp.broadcast_to(points[None], (team, owned, width))
    pts = lax.all_to_all(copies, AXES, 0, 0, axis_index_groups=TEAMS).reshape(team * owned, width)
    far = lax.ppermute(pts, AXES, CROSS)
    rows = team * owned
    half = jax.ShapeDtypeStruct((rows, 256), BF16)
    wide = jax.ShapeDtypeStruct((rows, 256), F32)
    narrow = jax.ShapeDtypeStruct((rows, 128), F32)

    tiles = slab.shape[0] // TILE
    held = [pltpu.VMEM((tiles, TILE, width), F32), pltpu.SemaphoreType.DMA((tiles,))]
    slab_later, _ = lax.optimization_barrier((slab, pts))
    other = lax.ppermute(slab_later, AXES, SWAP)
    own = call(own_kernel, (half, half, wide, narrow), COST[0], pts, slab, hbm=(1,), scratch=held)
    far, _ = lax.optimization_barrier((far, own[3]))
    far_other = lax.ppermute(far, AXES, SWAP)
    left = own[:2]
    vec, tot = call(other_kernel, (wide, narrow), COST[1], *own, other)
    block = jax.ShapeDtypeStruct((team, owned + 1, 1, width), F32)
    pair = functools.partial(pair_kernel, ratio)
    part = call(pair, block, 1 << 28, pts, *left, far, far_other, vec, tot)
    parts = lax.all_to_all(part, AXES, 0, 0, axis_index_groups=TEAMS)
    return call(final_kernel, jax.ShapeDtypeStruct((owned, width), F32), 1 << 16, parts)


def solution(mesh):
    placed = (P(("grp", "mem"), None), P("mem", None))
    return jax.shard_map(
        shards, mesh=mesh, in_specs=placed, out_specs=P(("grp", "mem"), None), check_vma=False
    )
```

```python
import functools

import jax
import jax.numpy as jnp
from jax import lax
from jax.experimental import pallas as pl
from jax.experimental.pallas import tpu as pltpu
from jax.sharding import PartitionSpec as P

F32, BF16 = jnp.float32, jnp.bfloat16
AXES = ("grp", "mem")
CHIPS_X, CHIPS_Y, Z_LO, Z_HI, CORES = 4, 8, 4, 2, 2
TILE = 512
COST = (1 << 20, 1 << 34, 1 << 31)


def place(index):
    group, member = divmod(index, CHIPS_Y * Z_HI * CORES)
    z_lo, x = divmod(group, CHIPS_X)
    y, rest = divmod(member, Z_HI * CORES)
    z_hi, core = divmod(rest, CORES)
    return x, y, z_hi * Z_LO + z_lo, core


def index_of(x, y, z, core):
    z_hi, z_lo = divmod(z, Z_LO)
    return (z_lo * CHIPS_X + x) * CHIPS_Y * Z_HI * CORES + (y * Z_HI + z_hi) * CORES + core


def team_of(z):
    return z if z < Z_LO else (z - Z_LO) ^ 2


DEVICES = range(CHIPS_X * CHIPS_Y * Z_LO * Z_HI * CORES)
TEAMS = {}
for _i in DEVICES:
    _x, _y, _z, _c = place(_i)
    TEAMS.setdefault((_x, team_of(_z), _c), []).append(_i)


def rank(index):
    _, y, z, _ = place(index)
    return z < Z_LO, (y - 4) % CHIPS_Y


TEAMS = [sorted(team, key=rank) for team in TEAMS.values()]

X_ORDER = ((2, 1, 0, 3), (1, 2, 3, 0), (0, 3, 2, 1), (3, 0, 1, 2))
Z_ORDER = ((0, 2, 1, 3, 4, 6, 5, 7), (1, 3, 0, 2, 5, 7, 4, 6))
CROSS = []
for _i in DEVICES:
    _x, _y, _z, _c = place(_i)
    _far = X_ORDER[_y % CHIPS_X][_x], _y, Z_ORDER[_y // CHIPS_X][_z], _c
    CROSS.append((index_of(*_far), _i))
SWAP = [(i, i ^ 1) for i in DEVICES]


def split2(v):
    hi = v.astype(BF16)
    return hi, (v - hi.astype(F32)).astype(BF16)


def split3(v):
    hi = v.astype(BF16).astype(F32)
    mid = (v - hi).astype(BF16).astype(F32)
    return hi, mid, v - hi - mid


def columns(first, second):
    ref = second if first is None else first
    lane = lax.broadcasted_iota(jnp.int32, (ref.shape[0], 128), 1)
    out = jnp.where(lane < 6, 1.0, 0.0).astype(F32)
    for at, col in ((0, first), (3, second)):
        if col is not None:
            for k, part in enumerate(split3(col)):
                out = jnp.where(lane == at + k, part, out)
    return out.astype(BF16)


NT = (((1,), (1,)), ((), ()))


def left_operands(pts):
    hi, lo = split2(-2.0 * pts)
    norm = jnp.sum(pts * pts, axis=1, keepdims=True) + 1.0
    return jnp.concatenate([hi, hi], axis=1), jnp.concatenate([lo, columns(None, norm)], axis=1)


def accumulate(left, rows, state):
    vec, tot = state
    hi, lo = split2(rows)
    norm = jnp.sum(rows * rows, axis=1, keepdims=True)
    both = jnp.concatenate([hi, lo], axis=1)
    extra = jnp.concatenate([hi, columns(norm, None)], axis=1)
    d = lax.dot_general(left[0], both, NT, preferred_element_type=F32)
    d = d + lax.dot_general(left[1], extra, NT, preferred_element_type=F32)
    w = lax.rsqrt(jnp.maximum(d, 1.0))
    w_hi, w_lo = split2(w)
    part = jnp.dot(w_hi, both, preferred_element_type=F32)
    part = part + jnp.dot(w_lo, both, preferred_element_type=F32)
    vec = vec + part
    for k in range(rows.shape[0] // 128):
        tot = tot + w[:, 128 * k : 128 * (k + 1)]
    return vec, tot


def zeros(rows):
    return jnp.zeros((rows, 256), F32), jnp.zeros((rows, 128), F32)


def add_tiles(left, state, slab_ref, tiles):
    for t in tiles:
        state = accumulate(left, slab_ref[t * TILE : (t + 1) * TILE, :], state)
    return state


def left_kernel(pts_ref, slab_ref, left1_ref, left2_ref):
    del slab_ref
    left1_ref[...], left2_ref[...] = left_operands(pts_ref[...])


def own_kernel(left1_ref, left2_ref, slab_ref, vec_ref, tot_ref):
    left = left1_ref[...], left2_ref[...]
    tiles = range(slab_ref.shape[0] // TILE)
    vec_ref[...], tot_ref[...] = add_tiles(left, zeros(left[0].shape[0]), slab_ref, tiles)


def other_kernel(left1_ref, left2_ref, vec_in, tot_in, slab_ref, vec_ref, tot_ref):
    left, state = (left1_ref[...], left2_ref[...]), (vec_in[...], tot_in[...])
    tiles = range(slab_ref.shape[0] // TILE)
    vec_ref[...], tot_ref[...] = add_tiles(left, state, slab_ref, tiles)


def pair_kernel(ratio, pts_ref, left1_ref, left2_ref, first_ref, second_ref, vec_ref, tot_ref, out_ref):
    pts = pts_ref[...]
    left = left1_ref[...], left2_ref[...]
    state = zeros(pts.shape[0])
    for ref in (first_ref, second_ref):
        state = accumulate(left, ref[...], state)
    pair_sum = jnp.sum(state[1], axis=1, keepdims=True)
    repel = pts * pair_sum - (state[0][:, :128] + state[0][:, 128:])
    numer = ratio * repel + (vec_ref[:, :128] + vec_ref[:, 128:])
    weight = jnp.sum(tot_ref[...], axis=1, keepdims=True)
    spread = jnp.where(lax.broadcasted_iota(jnp.int32, (256, 128), 0) % 16 == lax.broadcasted_iota(jnp.int32, (256, 128), 1), weight, 0.0)
    for k in range(out_ref.shape[0]):
        at = 16 * k
        out_ref[k, 0:16, 0, :] = numer[at : at + 16]
        out_ref[k, 16, 0, :] = jnp.sum(spread[at : at + 16], axis=0)


def final_kernel(parts_ref, out_ref):
    total = parts_ref[0, :, 0, :]
    for k in range(1, parts_ref.shape[0]):
        total = total + parts_ref[k, :, 0, :]
    rows = lax.broadcasted_iota(jnp.int32, (16, 128), 0)
    lanes = lax.broadcasted_iota(jnp.int32, (16, 128), 1)
    weight = jnp.sum(jnp.where(rows == lanes, total[16:17], 0.0), axis=1, keepdims=True)
    out_ref[...] = total[0:16] / weight


def call(kernel, shapes, flops, *args, hbm=()):
    args = [pltpu.with_memory_space_constraint(a, pltpu.HBM) if k in hbm else a for k, a in enumerate(args)]
    spaces = [pltpu.HBM if k in hbm else pltpu.VMEM for k in range(len(args))]
    return pl.pallas_call(
        kernel,
        out_shape=shapes,
        in_specs=[pl.BlockSpec(memory_space=space) for space in spaces],
        out_specs=jax.tree.map(lambda _: pl.BlockSpec(memory_space=pltpu.VMEM), shapes),
        cost_estimate=pl.CostEstimate(flops=flops, bytes_accessed=1 << 10, transcendentals=1),
        compiler_params=pltpu.CompilerParams(vmem_limit_bytes=24 << 20),
    )(*args)


def shards(points, slab):
    owned, width = points.shape
    team = len(TEAMS[0])
    ratio = slab.shape[0] / (owned * lax.axis_size("grp"))
    copies = jnp.broadcast_to(points[None], (team, owned, width))
    pts = lax.all_to_all(copies, AXES, 0, 0, axis_index_groups=TEAMS).reshape(team * owned, width)
    far = lax.ppermute(pts, AXES, CROSS)
    rows = team * owned
    half = jax.ShapeDtypeStruct((rows, 256), BF16)
    wide = jax.ShapeDtypeStruct((rows, 256), F32)
    narrow = jax.ShapeDtypeStruct((rows, 128), F32)

    left = call(left_kernel, (half, half), COST[0], pts, slab, hbm=(1,))
    slab_later, _ = lax.optimization_barrier((slab, left[0]))
    other = lax.ppermute(slab_later, AXES, SWAP)
    vec, tot = call(own_kernel, (wide, narrow), COST[1], *left, slab)
    far, _ = lax.optimization_barrier((far, tot))
    far_other = lax.ppermute(far, AXES, SWAP)
    vec, tot = call(other_kernel, (wide, narrow), COST[2], *left, vec, tot, other)
    block = jax.ShapeDtypeStruct((team, owned + 1, 1, width), F32)
    pair = functools.partial(pair_kernel, ratio)
    part = call(pair, block, 1 << 28, pts, *left, far, far_other, vec, tot)
    parts = lax.all_to_all(part, AXES, 0, 0, axis_index_groups=TEAMS)
    return call(final_kernel, jax.ShapeDtypeStruct((owned, width), F32), 1 << 16, parts)


def solution(mesh):
    placed = (P(("grp", "mem"), None), P("mem", None))
    return jax.shard_map(
        shards, mesh=mesh, in_specs=placed, out_specs=P(("grp", "mem"), None), check_vma=False
    )
```

```python
import functools

import jax
import jax.numpy as jnp
from jax import lax
from jax.experimental import pallas as pl
from jax.experimental.pallas import tpu as pltpu
from jax.sharding import PartitionSpec as P

F32, BF16 = jnp.float32, jnp.bfloat16
AXES = ("grp", "mem")
CHIPS_X, CHIPS_Y, Z_LO, Z_HI, CORES = 4, 8, 4, 2, 2
COST = (1 << 20, 1 << 34, 1 << 31)


def place(index):
    group, member = divmod(index, CHIPS_Y * Z_HI * CORES)
    z_lo, x = divmod(group, CHIPS_X)
    y, rest = divmod(member, Z_HI * CORES)
    z_hi, core = divmod(rest, CORES)
    return x, y, z_hi * Z_LO + z_lo, core


def index_of(x, y, z, core):
    z_hi, z_lo = divmod(z, Z_LO)
    return (z_lo * CHIPS_X + x) * CHIPS_Y * Z_HI * CORES + (y * Z_HI + z_hi) * CORES + core


def team_of(z):
    return z if z < Z_LO else (z - Z_LO) ^ 2


DEVICES = range(CHIPS_X * CHIPS_Y * Z_LO * Z_HI * CORES)
TEAMS = {}
for _i in DEVICES:
    _x, _y, _z, _c = place(_i)
    TEAMS.setdefault((_x, team_of(_z), _c), []).append(_i)


def rank(index):
    _, y, z, _ = place(index)
    return z < Z_LO, (y - 4) % CHIPS_Y


TEAMS = [sorted(team, key=rank) for team in TEAMS.values()]

X_FAR = ((2, 1, 0, 3), (1, 2, 3, 0), (0, 3, 2, 1), (3, 0, 1, 2))
X_NEAR = ((3, 0, 1, 2), (0, 3, 2, 1), (1, 2, 3, 0), (2, 1, 0, 3))
Z_FAR, Z_NEAR = (1, 3, 0, 2, 5, 7, 4, 6), (0, 2, 1, 3, 4, 6, 5, 7)


def cross(x_orders, z_order):
    pairs = []
    for i in DEVICES:
        x, y, z, core = place(i)
        flip, step = divmod(y, CHIPS_X)
        pairs.append((index_of(x_orders[step][x], y, z_order[z], core ^ flip), i))
    return pairs


FAR, NEAR = cross(X_FAR, Z_FAR), cross(X_NEAR, Z_NEAR)
SWAP = [(i, i ^ 1) for i in DEVICES]


def split2(v):
    hi = v.astype(BF16)
    return hi, (v - hi.astype(F32)).astype(BF16)


def split3(v):
    hi = v.astype(BF16).astype(F32)
    mid = (v - hi).astype(BF16).astype(F32)
    return hi, mid, v - hi - mid


def columns(first, second):
    ref = second if first is None else first
    lane = lax.broadcasted_iota(jnp.int32, (ref.shape[0], 128), 1)
    out = jnp.where(lane < 6, 1.0, 0.0).astype(F32)
    for at, col in ((0, first), (3, second)):
        if col is not None:
            for k, part in enumerate(split3(col)):
                out = jnp.where(lane == at + k, part, out)
    return out.astype(BF16)


NT = (((1,), (1,)), ((), ()))


def left_operands(pts):
    hi, lo = split2(-2.0 * pts)
    norm = jnp.sum(pts * pts, axis=1, keepdims=True) + 1.0
    return jnp.concatenate([hi, hi], axis=1), jnp.concatenate([lo, columns(None, norm)], axis=1)


def sums_of(left, rows):
    hi, lo = split2(rows)
    norm = jnp.sum(rows * rows, axis=1, keepdims=True)
    both = jnp.concatenate([hi, lo], axis=1)
    extra = jnp.concatenate([hi, columns(norm, None)], axis=1)
    d = lax.dot_general(left[0], both, NT, preferred_element_type=F32)
    d = d + lax.dot_general(left[1], extra, NT, preferred_element_type=F32)
    w = lax.rsqrt(jnp.maximum(d, 1.0))
    w_hi, w_lo = split2(w)
    count = w.shape[0]
    vec = jnp.zeros((count, both.shape[1]), F32)
    for at in range(0, rows.shape[0], 256):
        part = jnp.concatenate([w_hi[:, at : at + 256], w_lo[:, at : at + 256]], axis=0)
        part = jnp.dot(part, both[at : at + 256], preferred_element_type=F32)
        vec = vec + (part[:count] + part[count:])
    tot = w[:, 0:128]
    for at in range(128, rows.shape[0], 128):
        tot = tot + w[:, at : at + 128]
    return vec[:, :128] + vec[:, 128:], tot


def left_kernel(pts_ref, slab_ref, left1_ref, left2_ref):
    del slab_ref
    left1_ref[...], left2_ref[...] = left_operands(pts_ref[...])


def sums_kernel(left1_ref, left2_ref, rows_ref, vec_ref, tot_ref):
    vec_ref[...], tot_ref[...] = sums_of((left1_ref[...], left2_ref[...]), rows_ref[...])


def last_kernel(ratio, pts_ref, left1_ref, left2_ref, rows_ref, *refs):
    *sums, out_ref = refs
    own_vec, own_tot, other_vec, other_tot, far_vec, far_tot = (ref[...] for ref in sums)
    near_vec, near_tot = sums_of((left1_ref[...], left2_ref[...]), rows_ref[...])
    pair_sum = jnp.sum(far_tot + near_tot, axis=1, keepdims=True)
    repel = pts_ref[...] * pair_sum - (far_vec + near_vec)
    numer = ratio * repel + (own_vec + other_vec)
    weight = jnp.sum(own_tot + other_tot, axis=1, keepdims=True)
    points, lanes = (lax.broadcasted_iota(jnp.int32, numer.shape, k) for k in (0, 1))
    spread = jnp.where(points % 16 == lanes, weight, 0.0)
    for k in range(out_ref.shape[0]):
        at = 16 * k
        out_ref[k, 0:16, 0, :] = numer[at : at + 16]
        out_ref[k, 16, 0, :] = jnp.sum(spread[at : at + 16], axis=0)


def final_kernel(parts_ref, out_ref):
    total = parts_ref[0, :, 0, :]
    for k in range(1, parts_ref.shape[0]):
        total = total + parts_ref[k, :, 0, :]
    rows = lax.broadcasted_iota(jnp.int32, (16, 128), 0)
    lanes = lax.broadcasted_iota(jnp.int32, (16, 128), 1)
    weight = jnp.sum(jnp.where(rows == lanes, total[16:17], 0.0), axis=1, keepdims=True)
    out_ref[...] = total[0:16] / weight


def call(kernel, shapes, flops, *args, hbm=()):
    args = [pltpu.with_memory_space_constraint(a, pltpu.HBM) if k in hbm else a for k, a in enumerate(args)]
    spaces = [pltpu.HBM if k in hbm else pltpu.VMEM for k in range(len(args))]
    return pl.pallas_call(
        kernel,
        out_shape=shapes,
        in_specs=[pl.BlockSpec(memory_space=space) for space in spaces],
        out_specs=jax.tree.map(lambda _: pl.BlockSpec(memory_space=pltpu.VMEM), shapes),
        cost_estimate=pl.CostEstimate(flops=flops, bytes_accessed=1 << 10, transcendentals=1),
        compiler_params=pltpu.CompilerParams(vmem_limit_bytes=24 << 20),
    )(*args)


def shards(points, slab):
    owned, width = points.shape
    team = len(TEAMS[0])
    ratio = slab.shape[0] / (owned * lax.axis_size("grp"))
    copies = jnp.broadcast_to(points[None], (team, owned, width))
    pts = lax.all_to_all(copies, AXES, 0, 0, axis_index_groups=TEAMS).reshape(team * owned, width)
    far = lax.ppermute(pts, AXES, FAR)
    near = lax.ppermute(pts, AXES, NEAR)
    rows = team * owned
    half = jax.ShapeDtypeStruct((rows, 256), BF16)
    whole = jax.ShapeDtypeStruct((rows, width), F32)

    left = call(left_kernel, (half, half), COST[0], pts, slab, hbm=(1,))
    slab_later, _ = lax.optimization_barrier((slab, left[0]))
    other = lax.ppermute(slab_later, AXES, SWAP)
    own_sums = call(sums_kernel, (whole, whole), COST[1], *left, slab)
    far, _ = lax.optimization_barrier((far, own_sums[1]))
    far_sums = call(sums_kernel, (whole, whole), COST[2], *left, far)
    other, *far_sums = lax.optimization_barrier((other, *far_sums))
    other_sums = call(sums_kernel, (whole, whole), COST[2], *left, other)
    last = functools.partial(last_kernel, ratio)
    block = jax.ShapeDtypeStruct((team, owned + 1, 1, width), F32)
    part = call(last, block, 1 << 28, pts, *left, near, *own_sums, *other_sums, *far_sums)
    parts = lax.all_to_all(part, AXES, 0, 0, axis_index_groups=TEAMS)
    return call(final_kernel, jax.ShapeDtypeStruct((owned, width), F32), 1 << 16, parts)


def solution(mesh):
    placed = (P(("grp", "mem"), None), P("mem", None))
    return jax.shard_map(
        shards, mesh=mesh, in_specs=placed, out_specs=P(("grp", "mem"), None), check_vma=False
    )
```

```python
import functools

import jax
import jax.numpy as jnp
from jax import lax
from jax.experimental import pallas as pl
from jax.experimental.pallas import tpu as pltpu
from jax.sharding import PartitionSpec as P

F32, BF16 = jnp.float32, jnp.bfloat16
AXES = ("grp", "mem")
CHIPS_X, CHIPS_Y, Z_LO, Z_HI, CORES = 4, 8, 4, 2, 2
COST = (1 << 20, 1 << 34, 1 << 31)


def place(index):
    group, member = divmod(index, CHIPS_Y * Z_HI * CORES)
    z_lo, x = divmod(group, CHIPS_X)
    y, rest = divmod(member, Z_HI * CORES)
    z_hi, core = divmod(rest, CORES)
    return x, y, z_hi * Z_LO + z_lo, core


def index_of(x, y, z, core):
    z_hi, z_lo = divmod(z, Z_LO)
    return (z_lo * CHIPS_X + x) * CHIPS_Y * Z_HI * CORES + (y * Z_HI + z_hi) * CORES + core


def team_of(z):
    return z if z < Z_LO else (z - Z_LO) ^ 2


DEVICES = range(CHIPS_X * CHIPS_Y * Z_LO * Z_HI * CORES)
TEAMS = {}
for _i in DEVICES:
    _x, _y, _z, _c = place(_i)
    TEAMS.setdefault((_x, team_of(_z), _c), []).append(_i)


def rank(index):
    _, y, z, _ = place(index)
    return z < Z_LO, (y - 5) % CHIPS_Y


TEAMS = [sorted(team, key=rank) for team in TEAMS.values()]

X_FAR = ((2, 1, 0, 3), (1, 2, 3, 0), (0, 3, 2, 1), (3, 0, 1, 2))
X_NEAR = ((3, 0, 1, 2), (0, 3, 2, 1), (1, 2, 3, 0), (2, 1, 0, 3))
Z_FAR, Z_NEAR = (1, 3, 0, 2, 5, 7, 4, 6), (0, 2, 1, 3, 4, 6, 5, 7)


def cross(x_orders, z_order):
    pairs = []
    for i in DEVICES:
        x, y, z, core = place(i)
        flip, step = divmod(y, CHIPS_X)
        pairs.append((index_of(x_orders[step][x], y, z_order[z], core ^ flip), i))
    return pairs


FAR, NEAR = cross(X_FAR, Z_FAR), cross(X_NEAR, Z_NEAR)
SWAP = [(i, i ^ 1) for i in DEVICES]


def split2(v):
    hi = v.astype(BF16)
    return hi, (v - hi.astype(F32)).astype(BF16)


def split3(v):
    hi = v.astype(BF16).astype(F32)
    mid = (v - hi).astype(BF16).astype(F32)
    return hi, mid, v - hi - mid


def columns(first, second):
    ref = second if first is None else first
    lane = lax.broadcasted_iota(jnp.int32, (ref.shape[0], 128), 1)
    out = jnp.where(lane < 6, 1.0, 0.0).astype(F32)
    for at, col in ((0, first), (3, second)):
        if col is not None:
            for k, part in enumerate(split3(col)):
                out = jnp.where(lane == at + k, part, out)
    return out.astype(BF16)


NT = (((1,), (1,)), ((), ()))


def left_operands(pts):
    hi, lo = split2(-2.0 * pts)
    norm = jnp.sum(pts * pts, axis=1, keepdims=True) + 1.0
    return jnp.concatenate([hi, hi], axis=1), jnp.concatenate([lo, columns(None, norm)], axis=1)


def sums_of(left, rows):
    hi, lo = split2(rows)
    norm = jnp.sum(rows * rows, axis=1, keepdims=True)
    both = jnp.concatenate([hi, lo], axis=1)
    extra = jnp.concatenate([hi, columns(norm, None)], axis=1)
    d = lax.dot_general(left[0], both, NT, preferred_element_type=F32)
    d = d + lax.dot_general(left[1], extra, NT, preferred_element_type=F32)
    w = lax.rsqrt(jnp.maximum(d, 1.0))
    w_hi, w_lo = split2(w)
    count = w.shape[0]
    vec = jnp.zeros((count, both.shape[1]), F32)
    for at in range(0, rows.shape[0], 256):
        part = jnp.concatenate([w_hi[:, at : at + 256], w_lo[:, at : at + 256]], axis=0)
        part = jnp.dot(part, both[at : at + 256], preferred_element_type=F32)
        vec = vec + (part[:count] + part[count:])
    tot = w[:, 0:128]
    for at in range(128, rows.shape[0], 128):
        tot = tot + w[:, at : at + 128]
    return vec[:, :128] + vec[:, 128:], tot


def left_kernel(pts_ref, slab_ref, left1_ref, left2_ref):
    del slab_ref
    left1_ref[...], left2_ref[...] = left_operands(pts_ref[...])


def sums_kernel(left1_ref, left2_ref, rows_ref, vec_ref, tot_ref):
    vec_ref[...], tot_ref[...] = sums_of((left1_ref[...], left2_ref[...]), rows_ref[...])


def last_kernel(ratio, pts_ref, left1_ref, left2_ref, rows_ref, *refs):
    *sums, out_ref = refs
    own_vec, own_tot, other_vec, other_tot, far_vec, far_tot = (ref[...] for ref in sums)
    near_vec, near_tot = sums_of((left1_ref[...], left2_ref[...]), rows_ref[...])
    pair_sum = jnp.sum(far_tot + near_tot, axis=1, keepdims=True)
    repel = pts_ref[...] * pair_sum - (far_vec + near_vec)
    numer = ratio * repel + (own_vec + other_vec)
    weight = jnp.sum(own_tot + other_tot, axis=1, keepdims=True)
    points, lanes = (lax.broadcasted_iota(jnp.int32, numer.shape, k) for k in (0, 1))
    spread = jnp.where(points % 16 == lanes, weight, 0.0)
    for k in range(out_ref.shape[0]):
        at = 16 * k
        out_ref[k, 0:16, 0, :] = numer[at : at + 16]
        out_ref[k, 16, 0, :] = jnp.sum(spread[at : at + 16], axis=0)


def final_kernel(parts_ref, out_ref):
    total = parts_ref[0, :, 0, :]
    for k in range(1, parts_ref.shape[0]):
        total = total + parts_ref[k, :, 0, :]
    rows = lax.broadcasted_iota(jnp.int32, (16, 128), 0)
    lanes = lax.broadcasted_iota(jnp.int32, (16, 128), 1)
    weight = jnp.sum(jnp.where(rows == lanes, total[16:17], 0.0), axis=1, keepdims=True)
    out_ref[...] = total[0:16] / weight


def call(kernel, shapes, flops, *args, hbm=()):
    args = [pltpu.with_memory_space_constraint(a, pltpu.HBM) if k in hbm else a for k, a in enumerate(args)]
    spaces = [pltpu.HBM if k in hbm else pltpu.VMEM for k in range(len(args))]
    return pl.pallas_call(
        kernel,
        out_shape=shapes,
        in_specs=[pl.BlockSpec(memory_space=space) for space in spaces],
        out_specs=jax.tree.map(lambda _: pl.BlockSpec(memory_space=pltpu.VMEM), shapes),
        cost_estimate=pl.CostEstimate(flops=flops, bytes_accessed=1 << 10, transcendentals=1),
        compiler_params=pltpu.CompilerParams(vmem_limit_bytes=24 << 20),
    )(*args)


def shards(points, slab):
    owned, width = points.shape
    team = len(TEAMS[0])
    ratio = slab.shape[0] / (owned * lax.axis_size("grp"))
    copies = jnp.broadcast_to(points[None], (team, owned, width))
    pts = lax.all_to_all(copies, AXES, 0, 0, axis_index_groups=TEAMS).reshape(team * owned, width)
    far = lax.ppermute(pts, AXES, FAR)
    near = lax.ppermute(pts, AXES, NEAR)
    rows = team * owned
    half = jax.ShapeDtypeStruct((rows, 256), BF16)
    whole = jax.ShapeDtypeStruct((rows, width), F32)

    left = call(left_kernel, (half, half), COST[0], pts, slab, hbm=(1,))
    slab_later, _ = lax.optimization_barrier((slab, left[0]))
    other = lax.ppermute(slab_later, AXES, SWAP)
    own_sums = call(sums_kernel, (whole, whole), COST[1], *left, slab)
    far, _ = lax.optimization_barrier((far, own_sums[1]))
    far_sums = call(sums_kernel, (whole, whole), COST[2], *left, far)
    other, *far_sums = lax.optimization_barrier((other, *far_sums))
    other_sums = call(sums_kernel, (whole, whole), COST[2], *left, other)
    last = functools.partial(last_kernel, ratio)
    block = jax.ShapeDtypeStruct((team, owned + 1, 1, width), F32)
    part = call(last, block, 1 << 28, pts, *left, near, *own_sums, *other_sums, *far_sums)
    parts = lax.all_to_all(part, AXES, 0, 0, axis_index_groups=TEAMS)
    return call(final_kernel, jax.ShapeDtypeStruct((owned, width), F32), 1 << 16, parts)


def solution(mesh):
    placed = (P(("grp", "mem"), None), P("mem", None))
    return jax.shard_map(
        shards, mesh=mesh, in_specs=placed, out_specs=P(("grp", "mem"), None), check_vma=False
    )
```

```python
import functools

import jax
import jax.numpy as jnp
from jax import lax
from jax.experimental import pallas as pl
from jax.experimental.pallas import tpu as pltpu
from jax.sharding import PartitionSpec as P

F32, BF16 = jnp.float32, jnp.bfloat16
AXES = ("grp", "mem")
CHIPS_X, CHIPS_Y, Z_LO, Z_HI, CORES = 4, 8, 4, 2, 2
COST = (1 << 20, 1 << 34, 1 << 31)


def place(index):
    group, member = divmod(index, CHIPS_Y * Z_HI * CORES)
    z_lo, x = divmod(group, CHIPS_X)
    y, rest = divmod(member, Z_HI * CORES)
    z_hi, core = divmod(rest, CORES)
    return x, y, z_hi * Z_LO + z_lo, core


def index_of(x, y, z, core):
    z_hi, z_lo = divmod(z, Z_LO)
    return (z_lo * CHIPS_X + x) * CHIPS_Y * Z_HI * CORES + (y * Z_HI + z_hi) * CORES + core


def team_of(z):
    return z if z < Z_LO else (z - Z_LO) ^ 2


DEVICES = range(CHIPS_X * CHIPS_Y * Z_LO * Z_HI * CORES)
TEAMS = {}
for _i in DEVICES:
    _x, _y, _z, _c = place(_i)
    TEAMS.setdefault((_x, team_of(_z), _c), []).append(_i)


def rank(index):
    _, y, z, _ = place(index)
    return z < Z_LO, (y - 5) % CHIPS_Y


TEAMS = [sorted(team, key=rank) for team in TEAMS.values()]

X_FAR = ((1, 2, 3, 0), (0, 3, 2, 1), (3, 0, 1, 2), (2, 1, 0, 3))
X_NEAR = ((0, 3, 2, 1), (1, 2, 3, 0), (2, 1, 0, 3), (3, 0, 1, 2))
Z_FAR, Z_NEAR = (1, 3, 0, 2, 5, 7, 4, 6), (0, 2, 1, 3, 4, 6, 5, 7)


def cross(x_orders, z_order):
    pairs = []
    for i in DEVICES:
        x, y, z, core = place(i)
        flip, step = divmod(y, CHIPS_X)
        pairs.append((index_of(x_orders[step][x], y, z_order[z], core ^ flip), i))
    return pairs


FAR, NEAR = cross(X_FAR, Z_FAR), cross(X_NEAR, Z_NEAR)
SWAP = [(i, i ^ 1) for i in DEVICES]


def split2(v):
    hi = v.astype(BF16)
    return hi, (v - hi.astype(F32)).astype(BF16)


def split3(v):
    hi = v.astype(BF16).astype(F32)
    mid = (v - hi).astype(BF16).astype(F32)
    return hi, mid, v - hi - mid


def columns(first, second):
    ref = second if first is None else first
    lane = lax.broadcasted_iota(jnp.int32, (ref.shape[0], 128), 1)
    out = jnp.where(lane < 6, 1.0, 0.0).astype(F32)
    for at, col in ((0, first), (3, second)):
        if col is not None:
            for k, part in enumerate(split3(col)):
                out = jnp.where(lane == at + k, part, out)
    return out.astype(BF16)


NT = (((1,), (1,)), ((), ()))


def left_operands(pts):
    hi, lo = split2(-2.0 * pts)
    norm = jnp.sum(pts * pts, axis=1, keepdims=True) + 1.0
    return jnp.concatenate([hi, hi], axis=1), jnp.concatenate([lo, columns(None, norm)], axis=1)


def sums_of(left, rows):
    hi, lo = split2(rows)
    norm = jnp.sum(rows * rows, axis=1, keepdims=True)
    both = jnp.concatenate([hi, lo], axis=1)
    extra = jnp.concatenate([hi, columns(norm, None)], axis=1)
    d = lax.dot_general(left[0], both, NT, preferred_element_type=F32)
    d = d + lax.dot_general(left[1], extra, NT, preferred_element_type=F32)
    w = lax.rsqrt(jnp.maximum(d, 1.0))
    w_hi, w_lo = split2(w)
    count = w.shape[0]
    vec = jnp.zeros((count, both.shape[1]), F32)
    for at in range(0, rows.shape[0], 256):
        part = jnp.concatenate([w_hi[:, at : at + 256], w_lo[:, at : at + 256]], axis=0)
        part = jnp.dot(part, both[at : at + 256], preferred_element_type=F32)
        vec = vec + (part[:count] + part[count:])
    tot = w[:, 0:128]
    for at in range(128, rows.shape[0], 128):
        tot = tot + w[:, at : at + 128]
    return vec[:, :128] + vec[:, 128:], tot


def left_kernel(pts_ref, slab_ref, left1_ref, left2_ref):
    del slab_ref
    left1_ref[...], left2_ref[...] = left_operands(pts_ref[...])


def sums_kernel(left1_ref, left2_ref, rows_ref, vec_ref, tot_ref):
    vec_ref[...], tot_ref[...] = sums_of((left1_ref[...], left2_ref[...]), rows_ref[...])


def last_kernel(ratio, pts_ref, left1_ref, left2_ref, rows_ref, *refs):
    *sums, out_ref = refs
    own_vec, own_tot, other_vec, other_tot, far_vec, far_tot = (ref[...] for ref in sums)
    near_vec, near_tot = sums_of((left1_ref[...], left2_ref[...]), rows_ref[...])
    pair_sum = jnp.sum(far_tot + near_tot, axis=1, keepdims=True)
    repel = pts_ref[...] * pair_sum - (far_vec + near_vec)
    numer = ratio * repel + (own_vec + other_vec)
    weight = jnp.sum(own_tot + other_tot, axis=1, keepdims=True)
    points, lanes = (lax.broadcasted_iota(jnp.int32, numer.shape, k) for k in (0, 1))
    spread = jnp.where(points % 16 == lanes, weight, 0.0)
    for k in range(out_ref.shape[0]):
        at = 16 * k
        out_ref[k, 0:16, 0, :] = numer[at : at + 16]
        out_ref[k, 16, 0, :] = jnp.sum(spread[at : at + 16], axis=0)


def final_kernel(parts_ref, out_ref):
    total = parts_ref[0, :, 0, :]
    for k in range(1, parts_ref.shape[0]):
        total = total + parts_ref[k, :, 0, :]
    rows = lax.broadcasted_iota(jnp.int32, (16, 128), 0)
    lanes = lax.broadcasted_iota(jnp.int32, (16, 128), 1)
    weight = jnp.sum(jnp.where(rows == lanes, total[16:17], 0.0), axis=1, keepdims=True)
    out_ref[...] = total[0:16] / weight


def call(kernel, shapes, flops, *args, hbm=()):
    args = [pltpu.with_memory_space_constraint(a, pltpu.HBM) if k in hbm else a for k, a in enumerate(args)]
    spaces = [pltpu.HBM if k in hbm else pltpu.VMEM for k in range(len(args))]
    return pl.pallas_call(
        kernel,
        out_shape=shapes,
        in_specs=[pl.BlockSpec(memory_space=space) for space in spaces],
        out_specs=jax.tree.map(lambda _: pl.BlockSpec(memory_space=pltpu.VMEM), shapes),
        cost_estimate=pl.CostEstimate(flops=flops, bytes_accessed=1 << 10, transcendentals=1),
        compiler_params=pltpu.CompilerParams(vmem_limit_bytes=24 << 20),
    )(*args)


def shards(points, slab):
    owned, width = points.shape
    team = len(TEAMS[0])
    ratio = slab.shape[0] / (owned * lax.axis_size("grp"))
    copies = jnp.broadcast_to(points[None], (team, owned, width))
    pts = lax.all_to_all(copies, AXES, 0, 0, axis_index_groups=TEAMS).reshape(team * owned, width)
    far = lax.ppermute(pts, AXES, FAR)
    near = lax.ppermute(pts, AXES, NEAR)
    rows = team * owned
    half = jax.ShapeDtypeStruct((rows, 256), BF16)
    whole = jax.ShapeDtypeStruct((rows, width), F32)

    left = call(left_kernel, (half, half), COST[0], pts, slab, hbm=(1,))
    slab_later, _ = lax.optimization_barrier((slab, left[0]))
    other = lax.ppermute(slab_later, AXES, SWAP)
    own_sums = call(sums_kernel, (whole, whole), COST[1], *left, slab)
    far, _ = lax.optimization_barrier((far, own_sums[1]))
    far_sums = call(sums_kernel, (whole, whole), COST[2], *left, far)
    other, *far_sums = lax.optimization_barrier((other, *far_sums))
    other_sums = call(sums_kernel, (whole, whole), COST[2], *left, other)
    last = functools.partial(last_kernel, ratio)
    block = jax.ShapeDtypeStruct((team, owned + 1, 1, width), F32)
    part = call(last, block, 1 << 28, pts, *left, near, *own_sums, *other_sums, *far_sums)
    parts = lax.all_to_all(part, AXES, 0, 0, axis_index_groups=TEAMS)
    return call(final_kernel, jax.ShapeDtypeStruct((owned, width), F32), 1 << 16, parts)


def solution(mesh):
    placed = (P(("grp", "mem"), None), P("mem", None))
    return jax.shard_map(
        shards, mesh=mesh, in_specs=placed, out_specs=P(("grp", "mem"), None), check_vma=False
    )
```

```python
import functools

import jax
import jax.numpy as jnp
from jax import lax
from jax.experimental import pallas as pl
from jax.experimental.pallas import tpu as pltpu
from jax.sharding import PartitionSpec as P

F32, BF16 = jnp.float32, jnp.bfloat16
AXES = ("grp", "mem")
CHIPS_X, CHIPS_Y, Z_LO, Z_HI, CORES = 4, 8, 4, 2, 2
COST = (1 << 20, 1 << 34, 1 << 31)


def place(index):
    group, member = divmod(index, CHIPS_Y * Z_HI * CORES)
    z_lo, x = divmod(group, CHIPS_X)
    y, rest = divmod(member, Z_HI * CORES)
    z_hi, core = divmod(rest, CORES)
    return x, y, z_hi * Z_LO + z_lo, core


def index_of(x, y, z, core):
    z_hi, z_lo = divmod(z, Z_LO)
    return (z_lo * CHIPS_X + x) * CHIPS_Y * Z_HI * CORES + (y * Z_HI + z_hi) * CORES + core


def team_of(z):
    return z if z < Z_LO else (z - Z_LO) ^ 2


DEVICES = range(CHIPS_X * CHIPS_Y * Z_LO * Z_HI * CORES)
TEAMS = {}
for _i in DEVICES:
    _x, _y, _z, _c = place(_i)
    TEAMS.setdefault((_x, team_of(_z), _c), []).append(_i)


def rank(index):
    _, y, z, _ = place(index)
    return z < Z_LO, (y - 5) % CHIPS_Y


TEAMS = [sorted(team, key=rank) for team in TEAMS.values()]

X_FAR = ((1, 2, 3, 0), (0, 3, 2, 1), (3, 0, 1, 2), (2, 1, 0, 3))
X_NEAR = ((0, 3, 2, 1), (1, 2, 3, 0), (2, 1, 0, 3), (3, 0, 1, 2))
Z_FAR, Z_NEAR = (2, 0, 3, 1, 6, 4, 7, 5), (0, 2, 1, 3, 4, 6, 5, 7)


def cross(x_orders, z_order):
    pairs = []
    for i in DEVICES:
        x, y, z, core = place(i)
        flip, step = divmod(y, CHIPS_X)
        pairs.append((index_of(x_orders[step][x], y, z_order[z], core ^ flip), i))
    return pairs


FAR, NEAR = cross(X_FAR, Z_FAR), cross(X_NEAR, Z_NEAR)
SWAP = [(i, i ^ 1) for i in DEVICES]


def split2(v):
    hi = v.astype(BF16)
    return hi, (v - hi.astype(F32)).astype(BF16)


def split3(v):
    hi = v.astype(BF16).astype(F32)
    mid = (v - hi).astype(BF16).astype(F32)
    return hi, mid, v - hi - mid


def columns(first, second):
    ref = second if first is None else first
    lane = lax.broadcasted_iota(jnp.int32, (ref.shape[0], 128), 1)
    out = jnp.where(lane < 6, 1.0, 0.0).astype(F32)
    for at, col in ((0, first), (3, second)):
        if col is not None:
            for k, part in enumerate(split3(col)):
                out = jnp.where(lane == at + k, part, out)
    return out.astype(BF16)


NT = (((1,), (1,)), ((), ()))


def left_operands(pts):
    hi, lo = split2(-2.0 * pts)
    norm = jnp.sum(pts * pts, axis=1, keepdims=True) + 1.0
    return jnp.concatenate([hi, hi], axis=1), jnp.concatenate([lo, columns(None, norm)], axis=1)


def sums_of(left, rows):
    hi, lo = split2(rows)
    norm = jnp.sum(rows * rows, axis=1, keepdims=True)
    both = jnp.concatenate([hi, lo], axis=1)
    extra = jnp.concatenate([hi, columns(norm, None)], axis=1)
    d = lax.dot_general(left[0], both, NT, preferred_element_type=F32)
    d = d + lax.dot_general(left[1], extra, NT, preferred_element_type=F32)
    w = lax.rsqrt(jnp.maximum(d, 1.0))
    w_hi, w_lo = split2(w)
    count = w.shape[0]
    vec = jnp.zeros((count, both.shape[1]), F32)
    for at in range(0, rows.shape[0], 256):
        part = jnp.concatenate([w_hi[:, at : at + 256], w_lo[:, at : at + 256]], axis=0)
        part = jnp.dot(part, both[at : at + 256], preferred_element_type=F32)
        vec = vec + (part[:count] + part[count:])
    tot = w[:, 0:128]
    for at in range(128, rows.shape[0], 128):
        tot = tot + w[:, at : at + 128]
    return vec[:, :128] + vec[:, 128:], tot


def left_kernel(pts_ref, slab_ref, left1_ref, left2_ref):
    del slab_ref
    left1_ref[...], left2_ref[...] = left_operands(pts_ref[...])


def sums_kernel(left1_ref, left2_ref, rows_ref, vec_ref, tot_ref):
    vec_ref[...], tot_ref[...] = sums_of((left1_ref[...], left2_ref[...]), rows_ref[...])


def last_kernel(ratio, pts_ref, left1_ref, left2_ref, rows_ref, *refs):
    *sums, out_ref = refs
    own_vec, own_tot, other_vec, other_tot, far_vec, far_tot = (ref[...] for ref in sums)
    near_vec, near_tot = sums_of((left1_ref[...], left2_ref[...]), rows_ref[...])
    pair_sum = jnp.sum(far_tot + near_tot, axis=1, keepdims=True)
    repel = pts_ref[...] * pair_sum - (far_vec + near_vec)
    numer = ratio * repel + (own_vec + other_vec)
    weight = jnp.sum(own_tot + other_tot, axis=1, keepdims=True)
    points, lanes = (lax.broadcasted_iota(jnp.int32, numer.shape, k) for k in (0, 1))
    spread = jnp.where(points % 16 == lanes, weight, 0.0)
    for k in range(out_ref.shape[0]):
        at = 16 * k
        out_ref[k, 0:16, 0, :] = numer[at : at + 16]
        out_ref[k, 16, 0, :] = jnp.sum(spread[at : at + 16], axis=0)


def final_kernel(parts_ref, out_ref):
    total = parts_ref[0, :, 0, :]
    for k in range(1, parts_ref.shape[0]):
        total = total + parts_ref[k, :, 0, :]
    rows = lax.broadcasted_iota(jnp.int32, (16, 128), 0)
    lanes = lax.broadcasted_iota(jnp.int32, (16, 128), 1)
    weight = jnp.sum(jnp.where(rows == lanes, total[16:17], 0.0), axis=1, keepdims=True)
    out_ref[...] = total[0:16] / weight


def call(kernel, shapes, flops, *args, hbm=()):
    args = [pltpu.with_memory_space_constraint(a, pltpu.HBM) if k in hbm else a for k, a in enumerate(args)]
    spaces = [pltpu.HBM if k in hbm else pltpu.VMEM for k in range(len(args))]
    return pl.pallas_call(
        kernel,
        out_shape=shapes,
        in_specs=[pl.BlockSpec(memory_space=space) for space in spaces],
        out_specs=jax.tree.map(lambda _: pl.BlockSpec(memory_space=pltpu.VMEM), shapes),
        cost_estimate=pl.CostEstimate(flops=flops, bytes_accessed=1 << 10, transcendentals=1),
        compiler_params=pltpu.CompilerParams(vmem_limit_bytes=24 << 20),
    )(*args)


def shards(points, slab):
    owned, width = points.shape
    team = len(TEAMS[0])
    ratio = slab.shape[0] / (owned * lax.axis_size("grp"))
    copies = jnp.broadcast_to(points[None], (team, owned, width))
    pts = lax.all_to_all(copies, AXES, 0, 0, axis_index_groups=TEAMS).reshape(team * owned, width)
    far = lax.ppermute(pts, AXES, FAR)
    near = lax.ppermute(pts, AXES, NEAR)
    rows = team * owned
    half = jax.ShapeDtypeStruct((rows, 256), BF16)
    whole = jax.ShapeDtypeStruct((rows, width), F32)

    left = call(left_kernel, (half, half), COST[0], pts, slab, hbm=(1,))
    slab_later, _ = lax.optimization_barrier((slab, left[0]))
    other = lax.ppermute(slab_later, AXES, SWAP)
    own_sums = call(sums_kernel, (whole, whole), COST[1], *left, slab)
    far, _ = lax.optimization_barrier((far, own_sums[1]))
    far_sums = call(sums_kernel, (whole, whole), COST[2], *left, far)
    other, *far_sums = lax.optimization_barrier((other, *far_sums))
    other_sums = call(sums_kernel, (whole, whole), COST[2], *left, other)
    last = functools.partial(last_kernel, ratio)
    block = jax.ShapeDtypeStruct((team, owned + 1, 1, width), F32)
    part = call(last, block, 1 << 28, pts, *left, near, *own_sums, *other_sums, *far_sums)
    parts = lax.all_to_all(part, AXES, 0, 0, axis_index_groups=TEAMS)
    return call(final_kernel, jax.ShapeDtypeStruct((owned, width), F32), 1 << 16, parts)


def solution(mesh):
    placed = (P(("grp", "mem"), None), P("mem", None))
    return jax.shard_map(
        shards, mesh=mesh, in_specs=placed, out_specs=P(("grp", "mem"), None), check_vma=False
    )
```

```python
import functools

import jax
import jax.numpy as jnp
from jax import lax
from jax.experimental import pallas as pl
from jax.experimental.pallas import tpu as pltpu
from jax.sharding import PartitionSpec as P

F32, BF16 = jnp.float32, jnp.bfloat16
AXES = ("grp", "mem")
CHIPS_X, CHIPS_Y, Z_LO, Z_HI, CORES = 4, 8, 4, 2, 2
COST = (1 << 20, 1 << 34, 1 << 31)


def place(index):
    group, member = divmod(index, CHIPS_Y * Z_HI * CORES)
    z_lo, x = divmod(group, CHIPS_X)
    y, rest = divmod(member, Z_HI * CORES)
    z_hi, core = divmod(rest, CORES)
    return x, y, z_hi * Z_LO + z_lo, core


def index_of(x, y, z, core):
    z_hi, z_lo = divmod(z, Z_LO)
    return (z_lo * CHIPS_X + x) * CHIPS_Y * Z_HI * CORES + (y * Z_HI + z_hi) * CORES + core


def team_of(z):
    return z if z < Z_LO else (z - Z_LO) ^ 2


DEVICES = range(CHIPS_X * CHIPS_Y * Z_LO * Z_HI * CORES)
TEAMS = {}
for _i in DEVICES:
    _x, _y, _z, _c = place(_i)
    TEAMS.setdefault((_x, team_of(_z), _c), []).append(_i)


def rank(index):
    _, y, z, _ = place(index)
    return z < Z_LO, (y - 5) % CHIPS_Y


TEAMS = [sorted(team, key=rank) for team in TEAMS.values()]

X_FAR = ((1, 2, 3, 0), (0, 3, 2, 1), (3, 0, 1, 2), (2, 1, 0, 3))
X_NEAR = ((0, 3, 2, 1), (1, 2, 3, 0), (2, 1, 0, 3), (3, 0, 1, 2))
Z_FAR, Z_NEAR = (1, 3, 0, 2, 5, 6, 4, 7), (0, 2, 1, 3, 4, 7, 5, 6)


def cross(x_orders, z_order):
    pairs = []
    for i in DEVICES:
        x, y, z, core = place(i)
        flip, step = divmod(y, CHIPS_X)
        pairs.append((index_of(x_orders[step][x], y, z_order[z], core ^ flip), i))
    return pairs


FAR, NEAR = cross(X_FAR, Z_FAR), cross(X_NEAR, Z_NEAR)
SWAP = [(i, i ^ 1) for i in DEVICES]


def split2(v):
    hi = v.astype(BF16)
    return hi, (v - hi.astype(F32)).astype(BF16)


def split3(v):
    hi = v.astype(BF16).astype(F32)
    mid = (v - hi).astype(BF16).astype(F32)
    return hi, mid, v - hi - mid


def columns(first, second):
    ref = second if first is None else first
    lane = lax.broadcasted_iota(jnp.int32, (ref.shape[0], 128), 1)
    out = jnp.where(lane < 6, 1.0, 0.0).astype(F32)
    for at, col in ((0, first), (3, second)):
        if col is not None:
            for k, part in enumerate(split3(col)):
                out = jnp.where(lane == at + k, part, out)
    return out.astype(BF16)


NT = (((1,), (1,)), ((), ()))


def left_operands(pts):
    hi, lo = split2(-2.0 * pts)
    norm = jnp.sum(pts * pts, axis=1, keepdims=True) + 1.0
    return jnp.concatenate([hi, hi], axis=1), jnp.concatenate([lo, columns(None, norm)], axis=1)


def sums_of(left, rows):
    hi, lo = split2(rows)
    norm = jnp.sum(rows * rows, axis=1, keepdims=True)
    both = jnp.concatenate([hi, lo], axis=1)
    extra = jnp.concatenate([hi, columns(norm, None)], axis=1)
    d = lax.dot_general(left[0], both, NT, preferred_element_type=F32)
    d = d + lax.dot_general(left[1], extra, NT, preferred_element_type=F32)
    w = lax.rsqrt(jnp.maximum(d, 1.0))
    w_hi, w_lo = split2(w)
    count = w.shape[0]
    vec = jnp.zeros((count, both.shape[1]), F32)
    for at in range(0, rows.shape[0], 256):
        part = jnp.concatenate([w_hi[:, at : at + 256], w_lo[:, at : at + 256]], axis=0)
        part = jnp.dot(part, both[at : at + 256], preferred_element_type=F32)
        vec = vec + (part[:count] + part[count:])
    tot = w[:, 0:128]
    for at in range(128, rows.shape[0], 128):
        tot = tot + w[:, at : at + 128]
    return vec[:, :128] + vec[:, 128:], tot


def left_kernel(pts_ref, slab_ref, left1_ref, left2_ref):
    del slab_ref
    left1_ref[...], left2_ref[...] = left_operands(pts_ref[...])


def sums_kernel(left1_ref, left2_ref, rows_ref, vec_ref, tot_ref):
    vec_ref[...], tot_ref[...] = sums_of((left1_ref[...], left2_ref[...]), rows_ref[...])


def last_kernel(ratio, pts_ref, left1_ref, left2_ref, rows_ref, *refs):
    *sums, out_ref = refs
    own_vec, own_tot, other_vec, other_tot, far_vec, far_tot = (ref[...] for ref in sums)
    near_vec, near_tot = sums_of((left1_ref[...], left2_ref[...]), rows_ref[...])
    pair_sum = jnp.sum(far_tot + near_tot, axis=1, keepdims=True)
    repel = pts_ref[...] * pair_sum - (far_vec + near_vec)
    numer = ratio * repel + (own_vec + other_vec)
    weight = jnp.sum(own_tot + other_tot, axis=1, keepdims=True)
    points, lanes = (lax.broadcasted_iota(jnp.int32, numer.shape, k) for k in (0, 1))
    spread = jnp.where(points % 16 == lanes, weight, 0.0)
    for k in range(out_ref.shape[0]):
        at = 16 * k
        out_ref[k, 0:16, 0, :] = numer[at : at + 16]
        out_ref[k, 16, 0, :] = jnp.sum(spread[at : at + 16], axis=0)


def final_kernel(parts_ref, out_ref):
    total = parts_ref[0, :, 0, :]
    for k in range(1, parts_ref.shape[0]):
        total = total + parts_ref[k, :, 0, :]
    rows = lax.broadcasted_iota(jnp.int32, (16, 128), 0)
    lanes = lax.broadcasted_iota(jnp.int32, (16, 128), 1)
    weight = jnp.sum(jnp.where(rows == lanes, total[16:17], 0.0), axis=1, keepdims=True)
    out_ref[...] = total[0:16] / weight


def call(kernel, shapes, flops, *args, hbm=()):
    args = [pltpu.with_memory_space_constraint(a, pltpu.HBM) if k in hbm else a for k, a in enumerate(args)]
    spaces = [pltpu.HBM if k in hbm else pltpu.VMEM for k in range(len(args))]
    return pl.pallas_call(
        kernel,
        out_shape=shapes,
        in_specs=[pl.BlockSpec(memory_space=space) for space in spaces],
        out_specs=jax.tree.map(lambda _: pl.BlockSpec(memory_space=pltpu.VMEM), shapes),
        cost_estimate=pl.CostEstimate(flops=flops, bytes_accessed=1 << 10, transcendentals=1),
        compiler_params=pltpu.CompilerParams(vmem_limit_bytes=24 << 20),
    )(*args)


def shards(points, slab):
    owned, width = points.shape
    team = len(TEAMS[0])
    ratio = slab.shape[0] / (owned * lax.axis_size("grp"))
    copies = jnp.broadcast_to(points[None], (team, owned, width))
    pts = lax.all_to_all(copies, AXES, 0, 0, axis_index_groups=TEAMS).reshape(team * owned, width)
    far = lax.ppermute(pts, AXES, FAR)
    near = lax.ppermute(pts, AXES, NEAR)
    rows = team * owned
    half = jax.ShapeDtypeStruct((rows, 256), BF16)
    whole = jax.ShapeDtypeStruct((rows, width), F32)

    left = call(left_kernel, (half, half), COST[0], pts, slab, hbm=(1,))
    slab_later, _ = lax.optimization_barrier((slab, left[0]))
    other = lax.ppermute(slab_later, AXES, SWAP)
    own_sums = call(sums_kernel, (whole, whole), COST[1], *left, slab)
    far, _ = lax.optimization_barrier((far, own_sums[1]))
    far_sums = call(sums_kernel, (whole, whole), COST[2], *left, far)
    other, *far_sums = lax.optimization_barrier((other, *far_sums))
    other_sums = call(sums_kernel, (whole, whole), COST[2], *left, other)
    last = functools.partial(last_kernel, ratio)
    block = jax.ShapeDtypeStruct((team, owned + 1, 1, width), F32)
    part = call(last, block, 1 << 28, pts, *left, near, *own_sums, *other_sums, *far_sums)
    parts = lax.all_to_all(part, AXES, 0, 0, axis_index_groups=TEAMS)
    return call(final_kernel, jax.ShapeDtypeStruct((owned, width), F32), 1 << 16, parts)


def solution(mesh):
    placed = (P(("grp", "mem"), None), P("mem", None))
    return jax.shard_map(
        shards, mesh=mesh, in_specs=placed, out_specs=P(("grp", "mem"), None), check_vma=False
    )
```

```python
import functools

import jax
import jax.numpy as jnp
from jax import lax
from jax.experimental import pallas as pl
from jax.experimental.pallas import tpu as pltpu
from jax.sharding import PartitionSpec as P

F32, BF16 = jnp.float32, jnp.bfloat16
AXES = ("grp", "mem")
CHIPS_X, CHIPS_Y, Z_LO, Z_HI, CORES = 4, 8, 4, 2, 2
COST = (1 << 20, 1 << 34, 1 << 31)


def place(index):
    group, member = divmod(index, CHIPS_Y * Z_HI * CORES)
    z_lo, x = divmod(group, CHIPS_X)
    y, rest = divmod(member, Z_HI * CORES)
    z_hi, core = divmod(rest, CORES)
    return x, y, z_hi * Z_LO + z_lo, core


def index_of(x, y, z, core):
    z_hi, z_lo = divmod(z, Z_LO)
    return (z_lo * CHIPS_X + x) * CHIPS_Y * Z_HI * CORES + (y * Z_HI + z_hi) * CORES + core


def team_of(z):
    return z if z < Z_LO else (z - Z_LO) ^ 2


DEVICES = range(CHIPS_X * CHIPS_Y * Z_LO * Z_HI * CORES)
TEAMS = {}
for _i in DEVICES:
    _x, _y, _z, _c = place(_i)
    TEAMS.setdefault((_x, team_of(_z), _c), []).append(_i)


def rank(index):
    _, y, z, _ = place(index)
    return z < Z_LO, (y - 5) % CHIPS_Y


TEAMS = [sorted(team, key=rank) for team in TEAMS.values()]

X_FAR = ((0, 3, 2, 1), (3, 0, 1, 2), (2, 1, 0, 3), (1, 2, 3, 0))
X_NEAR = ((1, 2, 3, 0), (2, 1, 0, 3), (3, 0, 1, 2), (0, 3, 2, 1))
Z_FAR, Z_NEAR = (1, 3, 0, 2, 5, 7, 4, 6), (0, 2, 1, 3, 4, 6, 5, 7)


def cross(x_orders, z_order):
    pairs = []
    for i in DEVICES:
        x, y, z, core = place(i)
        flip, step = divmod(y, CHIPS_X)
        pairs.append((index_of(x_orders[step][x], y, z_order[z], core ^ flip), i))
    return pairs


FAR, NEAR = cross(X_FAR, Z_FAR), cross(X_NEAR, Z_NEAR)
SWAP = [(i, i ^ 1) for i in DEVICES]


def split2(v):
    hi = v.astype(BF16)
    return hi, (v - hi.astype(F32)).astype(BF16)


def split3(v):
    hi = v.astype(BF16).astype(F32)
    mid = (v - hi).astype(BF16).astype(F32)
    return hi, mid, v - hi - mid


def columns(first, second):
    ref = second if first is None else first
    lane = lax.broadcasted_iota(jnp.int32, (ref.shape[0], 128), 1)
    out = jnp.where(lane < 6, 1.0, 0.0).astype(F32)
    for at, col in ((0, first), (3, second)):
        if col is not None:
            for k, part in enumerate(split3(col)):
                out = jnp.where(lane == at + k, part, out)
    return out.astype(BF16)


NT = (((1,), (1,)), ((), ()))


def left_operands(pts):
    hi, lo = split2(-2.0 * pts)
    norm = jnp.sum(pts * pts, axis=1, keepdims=True) + 1.0
    return jnp.concatenate([hi, hi], axis=1), jnp.concatenate([lo, columns(None, norm)], axis=1)


def sums_of(left, rows):
    hi, lo = split2(rows)
    norm = jnp.sum(rows * rows, axis=1, keepdims=True)
    both = jnp.concatenate([hi, lo], axis=1)
    extra = jnp.concatenate([hi, columns(norm, None)], axis=1)
    d = lax.dot_general(left[0], both, NT, preferred_element_type=F32)
    d = d + lax.dot_general(left[1], extra, NT, preferred_element_type=F32)
    w = lax.rsqrt(jnp.maximum(d, 1.0))
    w_hi, w_lo = split2(w)
    count = w.shape[0]
    vec = jnp.zeros((count, both.shape[1]), F32)
    for at in range(0, rows.shape[0], 256):
        part = jnp.concatenate([w_hi[:, at : at + 256], w_lo[:, at : at + 256]], axis=0)
        part = jnp.dot(part, both[at : at + 256], preferred_element_type=F32)
        vec = vec + (part[:count] + part[count:])
    tot = w[:, 0:128]
    for at in range(128, rows.shape[0], 128):
        tot = tot + w[:, at : at + 128]
    return vec[:, :128] + vec[:, 128:], tot


def left_kernel(pts_ref, slab_ref, left1_ref, left2_ref):
    del slab_ref
    left1_ref[...], left2_ref[...] = left_operands(pts_ref[...])


def sums_kernel(left1_ref, left2_ref, rows_ref, vec_ref, tot_ref):
    vec_ref[...], tot_ref[...] = sums_of((left1_ref[...], left2_ref[...]), rows_ref[...])


def last_kernel(ratio, pts_ref, left1_ref, left2_ref, rows_ref, *refs):
    *sums, out_ref = refs
    own_vec, own_tot, other_vec, other_tot, far_vec, far_tot = (ref[...] for ref in sums)
    near_vec, near_tot = sums_of((left1_ref[...], left2_ref[...]), rows_ref[...])
    pair_sum = jnp.sum(far_tot + near_tot, axis=1, keepdims=True)
    repel = pts_ref[...] * pair_sum - (far_vec + near_vec)
    numer = ratio * repel + (own_vec + other_vec)
    weight = jnp.sum(own_tot + other_tot, axis=1, keepdims=True)
    points, lanes = (lax.broadcasted_iota(jnp.int32, numer.shape, k) for k in (0, 1))
    spread = jnp.where(points % 16 == lanes, weight, 0.0)
    for k in range(out_ref.shape[0]):
        at = 16 * k
        out_ref[k, 0:16, 0, :] = numer[at : at + 16]
        out_ref[k, 16, 0, :] = jnp.sum(spread[at : at + 16], axis=0)


def final_kernel(parts_ref, out_ref):
    total = parts_ref[0, :, 0, :]
    for k in range(1, parts_ref.shape[0]):
        total = total + parts_ref[k, :, 0, :]
    rows = lax.broadcasted_iota(jnp.int32, (16, 128), 0)
    lanes = lax.broadcasted_iota(jnp.int32, (16, 128), 1)
    weight = jnp.sum(jnp.where(rows == lanes, total[16:17], 0.0), axis=1, keepdims=True)
    out_ref[...] = total[0:16] / weight


def call(kernel, shapes, flops, *args, hbm=()):
    args = [pltpu.with_memory_space_constraint(a, pltpu.HBM) if k in hbm else a for k, a in enumerate(args)]
    spaces = [pltpu.HBM if k in hbm else pltpu.VMEM for k in range(len(args))]
    return pl.pallas_call(
        kernel,
        out_shape=shapes,
        in_specs=[pl.BlockSpec(memory_space=space) for space in spaces],
        out_specs=jax.tree.map(lambda _: pl.BlockSpec(memory_space=pltpu.VMEM), shapes),
        cost_estimate=pl.CostEstimate(flops=flops, bytes_accessed=1 << 10, transcendentals=1),
        compiler_params=pltpu.CompilerParams(vmem_limit_bytes=24 << 20),
    )(*args)


def shards(points, slab):
    owned, width = points.shape
    team = len(TEAMS[0])
    ratio = slab.shape[0] / (owned * lax.axis_size("grp"))
    copies = jnp.broadcast_to(points[None], (team, owned, width))
    pts = lax.all_to_all(copies, AXES, 0, 0, axis_index_groups=TEAMS).reshape(team * owned, width)
    far = lax.ppermute(pts, AXES, FAR)
    near = lax.ppermute(pts, AXES, NEAR)
    rows = team * owned
    half = jax.ShapeDtypeStruct((rows, 256), BF16)
    whole = jax.ShapeDtypeStruct((rows, width), F32)

    left = call(left_kernel, (half, half), COST[0], pts, slab, hbm=(1,))
    slab_later, _ = lax.optimization_barrier((slab, left[0]))
    other = lax.ppermute(slab_later, AXES, SWAP)
    own_sums = call(sums_kernel, (whole, whole), COST[1], *left, slab)
    far, _ = lax.optimization_barrier((far, own_sums[1]))
    far_sums = call(sums_kernel, (whole, whole), COST[2], *left, far)
    other, *far_sums = lax.optimization_barrier((other, *far_sums))
    other_sums = call(sums_kernel, (whole, whole), COST[2], *left, other)
    last = functools.partial(last_kernel, ratio)
    block = jax.ShapeDtypeStruct((team, owned + 1, 1, width), F32)
    part = call(last, block, 1 << 28, pts, *left, near, *own_sums, *other_sums, *far_sums)
    parts = lax.all_to_all(part, AXES, 0, 0, axis_index_groups=TEAMS)
    return call(final_kernel, jax.ShapeDtypeStruct((owned, width), F32), 1 << 16, parts)


def solution(mesh):
    placed = (P(("grp", "mem"), None), P("mem", None))
    return jax.shard_map(
        shards, mesh=mesh, in_specs=placed, out_specs=P(("grp", "mem"), None), check_vma=False
    )
```
